512 devices in a mesh: visit: 8 (over y, core), sky: 64 (over x, z).
Axes of the slice: x: 4, y: 4, z: 16, core: 2. Of those that a mesh axis runs over, the one named last changes fastest.
Arguments:
- raw_tiles: float32 [28672, 128, 128], P(('visit', 'sky')), may hold values from -4 to 4
- warp_shift: int32 [28672, 2], P(('visit', 'sky')), may hold values from -2 to 2
- warp_taps: float32 [28672, 2, 4], P(('visit', 'sky')), may hold values from -0.25 to 1
- match_coeffs: float32 [28672, 27], P(('visit', 'sky')), may hold values from -3 to 3
- tile_weights: float32 [28672], P(('visit', 'sky')), may hold values from 0.5 to 2
- dest_owner: int32 [28672, 1], P(('visit', 'sky')), may hold values from 0 to 63; in each aligned block of 56 rows (0 to 55, 56 to 111, ...) at most 2 rows name the same one
- dest_cell: int32 [28672], P(('visit', 'sky')), may hold values from 0 to 15
- template: float32 [16384, 1024], P('sky'), may hold values from -6 to 6
- basis_rows: float32 [9, 31], replicated, may hold values from -1 to 1
- basis_cols: float32 [9, 31], replicated, may hold values from -1 to 1
Outputs:
- coadd: float32 [16384, 1024], P('sky', 'visit')
The draws below stay inside these ranges and needn't reach their ends.
Inputs may be any that keep to these rules, and one draw needn't show every extreme that they name: `dest_owner`: among the tiles of one device no owner is named more than 2 times, a bound that some block reaches.
All inputs are finite; a program needn't handle non-finite values.
Results may differ from the reference program's by a relative error of at most 0.0003.
Values sent between devices are 32-bit elements; how exact they have to be, the bound alone decides.
A program may use at most 128 MiB of HBM per device.

```python
import math
import jax
import jax.numpy as jnp
import numpy as np
from jax import lax

TS = 128
PH = 256
PW = 1024
KSIZE = 31
NBASIS = 9
TILES_DEV = 56
CAP = 2
CELLS = 16
TILES = 28672
PH_ALL = 16384
N_SKY = 64


def place_ends(array, key, smallest, largest):
    index_at = [jax.random.randint(jax.random.fold_in(key, axis), (), 0, length) for axis, length in enumerate(array.shape)]
    widest = array.shape.index(max(array.shape))
    neighbour = index_at[:widest] + [(index_at[widest] + 1) % array.shape[widest]] + index_at[widest + 1:]
    return array.at[tuple(index_at)].set(smallest).at[tuple(neighbour)].set(largest)


def block_levels(stream_key, dims, split, smallest, largest):
    def one(dim, blocks):
        heights = jax.random.uniform(jax.random.fold_in(jax.random.fold_in(stream_key, 6), dim), (blocks,), jnp.float32, smallest / len(split), largest / len(split))
        return jnp.repeat(jnp.exp(heights), dims[dim] // blocks).reshape((-1,) + (1,) * (len(dims) - dim - 1))

    level = one(*split[0])
    for cut in split[1:]:
        level = level * one(*cut)
    return level


def deal_out(key, own, number, rows, number_of, top, bound, lean):
    ranking = jax.random.permutation(key, number_of)
    heavy_load, usual = shares(number_of, rows * top, bound, lean, True), shares(number_of, rows * top, bound, lean, False)
    places = jnp.arange(number_of)

    def named(tallies, turn):
        used = int((tallies > 0).sum())
        fixed = max(1, used // 4)
        shifted = fixed + (places - fixed + turn * (used - fixed)) % max(1, number_of - fixed)
        return jnp.zeros((number_of,), jnp.int32).at[ranking[jnp.where(places < fixed, places, shifted)]].set(jnp.asarray(tallies, jnp.int32))

    tallies = jnp.where(number % 4 == 0, named(heavy_load, number // 4), named(usual, number - number // 4 - 1))
    mixed = jax.random.permutation(jax.random.fold_in(own, 3), number_of)
    source_of, taker = mixed[0:number_of // 2 * 2:2], mixed[1:number_of // 2 * 2:2]
    margin = jnp.minimum(tallies[source_of] - 1, bound - tallies[taker]) // 2
    margin = jnp.where((source_of == ranking[0]) | (taker == ranking[0]) | (tallies[taker] == 0), 0, jnp.maximum(margin, 0))
    shifted = jax.random.randint(jax.random.fold_in(own, 4), (number_of // 2,), 0, 1 << 20) % (margin + 1)
    tallies = tallies.at[source_of].add(-shifted).at[taker].add(shifted)
    members = jnp.searchsorted(jnp.cumsum(tallies), jnp.arange(rows * top), side="right").astype(jnp.int32)
    table = members.reshape(top, rows).T
    table = table[jax.random.permutation(jax.random.fold_in(own, 1), rows)]
    turn = jax.random.randint(jax.random.fold_in(own, 2), (rows, 1), 0, top)
    return jnp.take_along_axis(table, (jnp.arange(top)[None, :] + turn) % top, axis=1)


def shares(count, total, most, skew, full):
    portions = [(1 << 20) // math.isqrt(rank ** skew) + 1 for rank in range(1, count + 1)]
    largest = most if full else min(most, max(-(-total // count), total * portions[0] // sum(portions)))
    least = 1 if total - largest >= count - 1 else 0
    counts, spare = [largest] + [least] * (count - 1), total - largest - least * (count - 1)
    while spare > 0:
        candidates = [i for i in range(1, count) if counts[i] < largest] or [i for i in range(1, count) if counts[i] < most]
        mass, budget = sum([portions[i] for i in candidates]), spare
        for i in candidates:
            more = min(most - counts[i], max(1, budget * portions[i] // mass), spare)
            counts[i] = counts[i] + more
            spare = spare - more
    return np.array(counts)


def normal_values(stream_key, extent, deviation, bound, shards=(), kind=jnp.bfloat16):
    array = deviation * jax.random.normal(stream_key, extent, jnp.float32)
    if shards:
        array = array * block_levels(stream_key, extent, shards, -0.22, 0.18)
    return jnp.clip(array, -bound, bound).astype(kind)


def setup_inputs(seed: int = 0) -> dict:
    seeds = jax.random.split(jax.random.key(seed), 11)
    raw_tiles = normal_values(seeds[0], (TILES, TS, TS), 0.3, 4.0, ((0, 512),), jnp.float32)
    warp_shift = place_ends(jax.random.randint(seeds[1], (TILES, 2), -2, 3), jax.random.fold_in(seeds[1], 1), -2, 2).astype(jnp.int32)
    warp_taps = jnp.clip(-0.25 + 1.25 * jax.random.uniform(seeds[2], (TILES, 2, 4), jnp.float32) ** block_levels(seeds[2], (TILES, 2, 4), ((0, 512),), -0.2, 0.2), -0.25, 1.0)
    match_coeffs = normal_values(seeds[3], (TILES, 3 * NBASIS), 0.2, 3.0, ((0, 512),), jnp.float32)
    tile_weights = jnp.clip(jnp.exp(math.log(2.0) - 1.3862944 * jax.random.uniform(seeds[4], (TILES,), jnp.float32) ** block_levels(seeds[4], (TILES,), ((0, 512),), -0.2, 0.2)), 0.5, 2.0)
    dest_owner_keys = jax.random.split(jax.random.fold_in(seeds[5], 1), TILES // TILES_DEV)
    dest_owner_turns = jax.random.permutation(jax.random.fold_in(seeds[5], 3), TILES // TILES_DEV)
    dest_owner = jax.vmap(lambda own, number: deal_out(jax.random.fold_in(seeds[5], 2), own, number, TILES_DEV, N_SKY, 1, CAP, 2))(dest_owner_keys, dest_owner_turns).reshape((TILES, 1))
    dest_cell = place_ends(jax.random.randint(seeds[6], (TILES,), 0, CELLS), jax.random.fold_in(seeds[6], 1), 0, CELLS - 1).astype(jnp.int32)
    template = normal_values(seeds[7], (PH_ALL, PW), 1.0, 6.0, ((0, 64),), jnp.float32)
    basis_rows = normal_values(seeds[8], (NBASIS, KSIZE), KSIZE ** -0.5, 1.0, (), jnp.float32)
    basis_cols = normal_values(seeds[9], (NBASIS, KSIZE), KSIZE ** -0.5, 1.0, (), jnp.float32)
    return dict(raw_tiles=raw_tiles, warp_shift=warp_shift, warp_taps=warp_taps, match_coeffs=match_coeffs, tile_weights=tile_weights, dest_owner=dest_owner, dest_cell=dest_cell, template=template, basis_rows=basis_rows, basis_cols=basis_cols)


def warp_matrix(shift, taps, size):
    idx = jnp.arange(size, dtype=jnp.int32)
    offset = idx[None, None, :] - idx[None, :, None] - shift[:, None, None] + 1
    total = jnp.zeros(offset.shape, jnp.float32)
    for tap in range(taps.shape[1]):
        total = total + jnp.where(offset == tap, taps[:, tap][:, None, None], jnp.float32(0.0))
    return total


def smear(image, rows_k, cols_k):
    half = rows_k.shape[0] // 2
    inner = lax.conv_general_dilated(image[None, None], rows_k.reshape(1, 1, -1, 1), (1, 1), ((half, half), (0, 0)), precision=lax.Precision.HIGHEST)
    outer = lax.conv_general_dilated(inner, cols_k.reshape(1, 1, 1, -1), (1, 1), ((0, 0), (half, half)), precision=lax.Precision.HIGHEST)
    return outer[0, 0]


def reference(raw_tiles, warp_shift, warp_taps, match_coeffs, tile_weights, dest_owner, dest_cell, template, basis_rows, basis_cols):
    blocks = TILES // TILES_DEV
    segs = N_SKY * CELLS
    nb = basis_rows.shape[0]

    def accumulate(carry, item):
        raw, shift, taps, coef, weight, owner, cell = item
        m_rows = warp_matrix(shift[:, 0], taps[:, 0, :], TS)
        m_cols = warp_matrix(shift[:, 1], taps[:, 1, :], TS)
        warped = jnp.einsum('tik,tkl->til', m_rows, raw, precision=lax.Precision.HIGHEST)
        warped = jnp.einsum('til,tjl->tij', warped, m_cols, precision=lax.Precision.HIGHEST)
        seg = (owner[:, 0] * CELLS + cell).astype(jnp.int32)
        sci = jax.ops.segment_sum((warped * weight[:, None, None]).reshape(-1, TS * TS), seg, num_segments=segs)
        cf = jax.ops.segment_sum(coef * weight[:, None], seg, num_segments=segs)
        return (carry[0] + sci, carry[1] + cf), None

    items = (raw_tiles.reshape(blocks, TILES_DEV, TS, TS), warp_shift.reshape(blocks, TILES_DEV, 2),
             warp_taps.reshape(blocks, TILES_DEV, 2, 4), match_coeffs.reshape(blocks, TILES_DEV, -1),
             tile_weights.reshape(blocks, TILES_DEV), dest_owner.reshape(blocks, TILES_DEV, 1),
             dest_cell.reshape(blocks, TILES_DEV))
    init = (jnp.zeros((segs, TS * TS), jnp.float32), jnp.zeros((segs, 3 * nb), jnp.float32))
    (sci_cells, coef_cells), unused = lax.scan(accumulate, init, items)
    cr = PH // TS
    cc = PW // TS
    sci_img = sci_cells.reshape(N_SKY, cr, cc, TS, TS).transpose(0, 1, 3, 2, 4).reshape(N_SKY * PH, PW)
    table = coef_cells.reshape(N_SKY, cr, cc, nb, 3)
    coord = (2.0 * jnp.arange(TS).astype(jnp.float32) + 1.0) / TS - 1.0
    model = jnp.zeros((N_SKY, cr, TS, cc, TS), jnp.float32)
    for b in range(nb):
        conv = smear(template, basis_rows[b], basis_cols[b]).reshape(N_SKY, cr, TS, cc, TS)
        field = (table[:, :, None, :, None, b, 0] + table[:, :, None, :, None, b, 1] * coord[None, None, None, None, :]
                 + table[:, :, None, :, None, b, 2] * coord[None, None, :, None, None])
        model = model + conv * field
    return sci_img - model.reshape(N_SKY * PH, PW)
```

```python
import jax
import jax.numpy as jnp
from jax import lax
from jax.experimental import pallas as pl
from jax.experimental.pallas import tpu as pltpu
from jax.sharding import PartitionSpec as P

MESH = pl.DeviceIdType.MESH
F32 = jnp.float32
TS = 128
COUNT = 56
OWNERS = 64
NB = 9
KS = 31
NX = 4
NZ = 16
STEPS = 8
MSG = 2 * TS + 8
EXT = 288


def tables_kernel(owner, cell, weight, coef, index, meta, filled):
    meta[...] = jnp.zeros(meta.shape, F32)

    @pl.loop(0, OWNERS)
    def _(o):
        filled[o] = 0
        index[2 * o] = -1
        index[2 * o + 1] = -1

    @pl.loop(0, COUNT)
    def _(t):
        o = owner[t, 0]
        k = filled[o]
        filled[o] = k + 1
        index[2 * o + k] = t
        meta[o, pl.ds(k, 1), 0 : 3 * NB] = coef[pl.ds(t, 1), :] * weight[t]
        meta[o, pl.ds(2 + k, 1), :] = jnp.full((1, TS), cell[t].astype(F32))


def place(x, y, z, c):
    return (lax.rem(y, NX) * 2 + c, lax.rem(x, NX) * NZ + lax.rem(z, NZ))


def main_kernel(
    index,
    shift,
    taps,
    weight,
    meta,
    b_rows,
    b_cols,
    raw,
    template,
    out,
    rawpad,
    snd,
    rcv,
    ysnd,
    yrcv,
    zrcv,
    fin0,
    fin1,
    halo,
    ext,
    shifted,
    middle,
    conv,
    raw_sem,
    ext_sem,
    halo_ss,
    halo_rs,
    x_ss,
    x_rs,
    y_ss,
    y_rs,
    z_ss,
    z_rs,
    f_ss,
    f_rs,
):
    visit = lax.axis_index("visit")
    sky = lax.axis_index("sky")
    y, c = visit // 2, visit % 2
    x, z = sky // NZ, sky % NZ
    pos = jnp.where(c == 0, y, x)

    def along(step):
        return place(
            jnp.where(c == 0, x, x + step), jnp.where(c == 0, y + step, y), z, c
        )

    def remote(src, dst, ss, rs, to):
        return pltpu.make_async_remote_copy(
            src_ref=src, dst_ref=dst, send_sem=ss, recv_sem=rs, device_id=to, device_id_type=MESH
        )

    raw_copy = pltpu.make_async_copy(raw, rawpad.at[:, pl.ds(8, TS), :], raw_sem)
    raw_copy.start()

    def ext_copy(k):
        block = lax.rem(visit + 7 + k, 8)
        return pltpu.make_async_copy(
            template.at[:, pl.ds(pl.multiple_of(block * TS, TS), TS)],
            ext.at[pl.ds(16, 256), pl.ds(k * TS, TS)],
            ext_sem.at[k],
        )

    for k in range(3):
        ext_copy(k).start()

    barrier = pltpu.get_barrier_semaphore()
    up, down = lax.rem(sky + 1, OWNERS), lax.rem(sky + OWNERS - 1, OWNERS)
    greeted = [(visit, up), (visit, down), place(x, y, z + 1, c), place(x, y, z + NZ - 1, c), place(x, y, z, 1 - c)]
    for a in range(1, NX):
        for d in range(2):
            greeted += [place(x + a, y, z, d), place(x, y + a, z, d)]
    for to in greeted:
        pl.semaphore_signal(barrier, inc=1, device_id=to, device_id_type=MESH)

    @pl.when(x != y)
    def _():
        for d in range(2):
            pl.semaphore_signal(barrier, inc=1, device_id=place(y, x, z, d), device_id_type=MESH)

    blank = jnp.zeros((COUNT, 8, TS), F32)
    rawpad[:, 0:8, :] = blank
    rawpad[:, TS + 8 : TS + 16, :] = blank

    pl.semaphore_wait(barrier, len(greeted) + jnp.where(x != y, 2, 0))

    halo_up = remote(template.at[pl.ds(240, 16), :], halo.at[0], halo_ss.at[0], halo_rs.at[0], (visit, up))
    halo_down = remote(template.at[pl.ds(0, 16), :], halo.at[1], halo_ss.at[1], halo_rs.at[1], (visit, down))
    halo_up.start()
    halo_down.start()
    raw_copy.wait()

    lane = lax.broadcasted_iota(jnp.int32, (1, TS), 1)

    def warp(slot):
        found = index[slot]
        t = jnp.maximum(found, 0)
        w = jnp.where(found >= 0, weight[t], 0.0)
        rows = None
        for a in range(4):
            part = rawpad[t, pl.ds(shift[t, 0] + (7 + a), TS), :] * (taps[t, 0, a] * w)
            rows = part if rows is None else rows + part
        total = None
        for a in range(4):
            d = shift[t, 1] + (a - 1)
            factor = jnp.where(jnp.logical_and(lane + d >= 0, lane + d < TS), taps[t, 1, a], 0.0)
            part = pltpu.roll(rows, lax.rem(TS - d, TS), 1) * factor
            total = part if total is None else total + part
        return total

    def x_target(m):
        a, d = m // 2, m % 2
        return place(jnp.where(d == 0, x + a, x), jnp.where(d == 0, y, y + a), z, d)

    def x_copy(j, m):
        slot = m // 2 * 2 + c
        return remote(snd.at[j, m], rcv.at[j, slot], x_ss.at[j, m], x_rs.at[j, slot], x_target(m))

    def own_copy(j):
        return pltpu.make_async_copy(snd.at[j, c], rcv.at[j, c], x_rs.at[j, c])

    def send_tiles(j):
        @pl.loop(0, 8)
        def _(m):
            a, d = m // 2, m % 2
            owner_x = lax.rem(jnp.where(d == 0, x, y) + a, NX)
            owner_z = lax.rem(jnp.where(d == 0, z + 8 - j, z + 9 + j), NZ)
            owner = owner_x * NZ + owner_z
            for k in range(2):
                snd[j, m, k * TS : (k + 1) * TS, :] = warp(2 * owner + k)
            snd[j, m, 2 * TS : MSG, :] = meta[owner]

            @pl.when(m == c)
            def _():
                own_copy(j).start()

            @pl.when(m != c)
            def _():
                x_copy(j, m).start()

    def wait_tiles(j):
        @pl.loop(0, 8)
        def _(m):
            @pl.when(m == c)
            def _():
                own_copy(j).wait()

            @pl.when(m != c)
            def _():
                remote(snd.at[j, m], rcv.at[j, m], x_ss.at[j, m], x_rs.at[j, m], x_target(m)).wait_recv()

    sub = lax.broadcasted_iota(jnp.int32, (8, TS), 0)

    def gather_cells(j, h):
        for e in range(2):
            group = lax.rem(pos + (3 - h if e == 0 else 1 + h), NX)
            coefs = []
            for r in range(2):
                cell = (r * 8 + group * 2 + e).astype(F32)
                pixels, row = None, None
                for m in range(8):
                    for k in range(2):
                        named = rcv[j, m, 2 * TS + 2 + k : 2 * TS + 3 + k, :]
                        mask = jnp.where(named == cell, 1.0, 0.0)
                        part = rcv[j, m, k * TS : (k + 1) * TS, :] * mask
                        pixels = part if pixels is None else pixels + part
                        part = rcv[j, m, 2 * TS + k : 2 * TS + 1 + k, :] * mask
                        row = part if row is None else row + part
                ysnd[j, h, e, r * TS : (r + 1) * TS, :] = pixels
                coefs.append(row)
            ysnd[j, h, e, 2 * TS : MSG, :] = jnp.where(sub == 0, coefs[0], jnp.where(sub == 1, coefs[1], 0.0))

    def y_copy(j, h, e):
        return remote(
            ysnd.at[j, h, e], yrcv.at[j, h, e], y_ss.at[j, h, e], y_rs.at[j, h, e], along(1 if e == 0 else NX - 1)
        )

    def y_send(j, h):
        for e in range(2):
            y_copy(j, h, e).start()

    def y_take(j, h):
        for e in range(2):
            y_copy(j, h - 1, e).wait_recv()
            ysnd[j, h, e] = ysnd[j, h, e] + yrcv[j, h - 1, e]

    def z_copy(j):
        to = place(x, y, jnp.where(c == 0, z + 1, z + NZ - 1), c)
        return remote(ysnd.at[j, 3], zrcv.at[j], z_ss.at[j], z_rs.at[j], to)

    def finish(j):
        y_take(j, 3)

        @pl.when(j >= 1)
        def _():
            z_copy(j - 1).wait_recv()
            ysnd[j, 3] = ysnd[j, 3] + zrcv[j - 1]

        @pl.when(jnp.logical_or(c == 0, j < STEPS - 1))
        def _():
            z_copy(j).start()

    send_tiles(0)
    send_tiles(1)

    halo_up.wait_recv()
    halo_down.wait_recv()
    for k in range(3):
        ext_copy(k).wait()
    keep_up = jnp.where(sky > 0, 1.0, 0.0)
    keep_down = jnp.where(sky < OWNERS - 1, 1.0, 0.0)
    for k in range(3):
        block = pl.multiple_of(lax.rem(visit + 7 + k, 8) * TS, TS)
        cols = slice(k * TS, (k + 1) * TS)
        ext[0:16, cols] = halo[0, :, pl.ds(block, TS)] * keep_up
        ext[272:EXT, cols] = halo[1, :, pl.ds(block, TS)] * keep_down
    ext[:, 0:TS] = ext[:, 0:TS] * jnp.where(visit > 0, 1.0, 0.0)
    ext[:, 2 * TS :] = ext[:, 2 * TS :] * jnp.where(visit < 7, 1.0, 0.0)
    for v in range(KS):
        shifted[v] = ext[:, TS - 15 + v : 2 * TS - 15 + v]

    @pl.loop(0, NB)
    def _(b):
        total = shifted[0] * b_cols[b, 0]
        for v in range(1, KS):
            total = total + shifted[v] * b_cols[b, v]
        middle[...] = total
        total = middle[1:257, :] * b_rows[b, 0]
        for u in range(1, KS):
            total = total + middle[u + 1 : u + 257, :] * b_rows[b, u]
        conv[b] = total

    @pl.loop(0, STEPS)
    def _(j):
        wait_tiles(j)
        gather_cells(j, 0)
        y_send(j, 0)

        @pl.loop(1, 4)
        def _(h):
            gather_cells(j, h)

        @pl.when(j + 2 < STEPS)
        def _():
            send_tiles(j + 2)

        @pl.when(j >= 1)
        def _():
            finish(j - 1)

        for h in range(1, 3):
            y_take(j, h)
            y_send(j, h)

    last = STEPS - 1
    finish(last)

    to_sibling = remote(zrcv.at[last, 1], fin0, f_ss.at[0], f_rs.at[0], place(x, y, z, 1))
    to_even = remote(ysnd.at[last, 3, 0], fin1, f_ss.at[1], f_rs.at[1], place(y, x, z, 0))
    to_odd = remote(ysnd.at[last, 3, 1], fin1, f_ss.at[2], f_rs.at[1], place(y, x, z, 1))
    stay_odd = pltpu.make_async_copy(ysnd.at[last, 3, 1], fin1, f_rs.at[1])

    @pl.when(c == 0)
    def _():
        z_copy(last).wait_recv()
        to_sibling.start()
        fin0[...] = zrcv[last, 0]

    @pl.when(c == 1)
    def _():
        to_even.start()

        @pl.when(x != y)
        def _():
            to_odd.start()

        @pl.when(x == y)
        def _():
            stay_odd.start()

        to_sibling.wait_recv()

    @pl.when(jnp.logical_and(c == 1, x == y))
    def _():
        stay_odd.wait()

    @pl.when(jnp.logical_not(jnp.logical_and(c == 1, x == y)))
    def _():
        to_odd.wait_recv()

    xs = (2.0 * lane.astype(F32) + 1.0) / TS - 1.0
    ys = (2.0 * lax.broadcasted_iota(jnp.int32, (TS, 1), 0).astype(F32) + 1.0) / TS - 1.0
    ys = jnp.broadcast_to(ys, (TS, TS))
    for r in range(2):
        rows = slice(r * TS, (r + 1) * TS)
        coef = fin0[2 * TS + r : 2 * TS + r + 1, :] + fin1[2 * TS + r : 2 * TS + r + 1, :]
        total = fin0[rows, :] + fin1[rows, :]
        for b in range(NB):
            flat = coef[:, 3 * b : 3 * b + 1] + coef[:, 3 * b + 1 : 3 * b + 2] * xs
            field = flat + coef[:, 3 * b + 2 : 3 * b + 3] * ys
            total = total - conv[b, rows, :] * field
        out[rows, :] = total

    halo_up.wait_send()
    halo_down.wait_send()

    @pl.loop(0, STEPS)
    def _(j):
        @pl.loop(0, 8)
        def _(m):
            @pl.when(m != c)
            def _():
                x_copy(j, m).wait_send()

        for h in range(3):
            for e in range(2):
                y_copy(j, h, e).wait_send()

        @pl.when(jnp.logical_or(c == 0, j < STEPS - 1))
        def _():
            z_copy(j).wait_send()

    @pl.when(c == 0)
    def _():
        to_sibling.wait_send()

    @pl.when(c == 1)
    def _():
        to_even.wait_send()

        @pl.when(x != y)
        def _():
            to_odd.wait_send()


def body(
    raw_tiles,
    warp_shift,
    warp_taps,
    match_coeffs,
    tile_weights,
    dest_owner,
    dest_cell,
    template,
    basis_rows,
    basis_cols,
):
    smem = pl.BlockSpec(memory_space=pltpu.SMEM)
    vmem = pl.BlockSpec(memory_space=pltpu.VMEM)
    hbm = pl.BlockSpec(memory_space=pl.ANY)
    index, meta = pl.pallas_call(
        tables_kernel,
        out_shape=(
            jax.ShapeDtypeStruct((2 * OWNERS,), jnp.int32),
            jax.ShapeDtypeStruct((OWNERS, 8, TS), F32),
        ),
        in_specs=[smem, smem, smem, vmem],
        out_specs=(smem, vmem),
        scratch_shapes=[pltpu.SMEM((OWNERS,), jnp.int32)],
        name="tables",
    )(dest_owner, dest_cell, tile_weights, match_coeffs)
    dma = pltpu.SemaphoreType.DMA
    return pl.pallas_call(
        main_kernel,
        out_shape=jax.ShapeDtypeStruct((2 * TS, TS), F32),
        in_specs=[smem, smem, smem, smem, vmem, smem, smem, hbm, hbm],
        out_specs=vmem,
        scratch_shapes=[
            pltpu.VMEM((COUNT, TS + 16, TS), F32),
            pltpu.VMEM((STEPS, 8, MSG, TS), F32),
            pltpu.VMEM((STEPS, 8, MSG, TS), F32),
            pltpu.VMEM((STEPS, 4, 2, MSG, TS), F32),
            pltpu.VMEM((STEPS, 3, 2, MSG, TS), F32),
            pltpu.VMEM((STEPS, 2, MSG, TS), F32),
            pltpu.VMEM((MSG, TS), F32),
            pltpu.VMEM((MSG, TS), F32),
            pltpu.VMEM((2, 16, 8 * TS), F32),
            pltpu.VMEM((EXT, 3 * TS), F32),
            pltpu.VMEM((KS, EXT, TS), F32),
            pltpu.VMEM((EXT, TS), F32),
            pltpu.VMEM((NB, 2 * TS, TS), F32),
            dma,
            dma((3,)),
            dma((2,)),
            dma((2,)),
            dma((STEPS, 8)),
            dma((STEPS, 8)),
            dma((STEPS, 3, 2)),
            dma((STEPS, 3, 2)),
            dma((STEPS,)),
            dma((STEPS,)),
            dma((3,)),
            dma((2,)),
        ],
        compiler_params=pltpu.CompilerParams(
            collective_id=0, has_side_effects=True, vmem_limit_bytes=58 * 2**20
        ),
        name="exchange",
    )(index, warp_shift, warp_taps, tile_weights, meta, basis_rows, basis_cols, raw_tiles, template)


def solution(mesh):
    return jax.shard_map(
        body,
        mesh=mesh,
        in_specs=(
            P(("visit", "sky"), None, None),
            P(("visit", "sky"), None),
            P(("visit", "sky"), None, None),
            P(("visit", "sky"), None),
            P(("visit", "sky")),
            P(("visit", "sky"), None),
            P(("visit", "sky")),
            P("sky", None),
            P(),
            P(),
        ),
        out_specs=P("sky", "visit"),
        check_vma=False,
    )
```

```python
import jax
import jax.numpy as jnp
from jax import lax
from jax.experimental import pallas as pl
from jax.experimental.pallas import tpu as pltpu
from jax.sharding import PartitionSpec as P

MESH = pl.DeviceIdType.MESH
F32 = jnp.float32
TS = 128
COUNT = 56
OWNERS = 64
NB = 9
KS = 31
NX = 4
NZ = 16
STEPS = 8
MSG = 2 * TS + 8
CELL = TS + 8
EXT = 288


def tables_kernel(owner, cell, weight, coef, index, meta, filled, square, by_tile):
    meta[...] = jnp.zeros(meta.shape, F32)
    square[...] = jnp.zeros(square.shape, F32)
    square[0 : 3 * NB, 0:COUNT] = coef[...]
    by_tile[...] = square[...].T

    @pl.loop(0, OWNERS)
    def _(o):
        filled[o] = 0
        index[2 * o] = -1
        index[2 * o + 1] = -1

    @pl.loop(0, COUNT)
    def _(t):
        o = owner[0, t]
        k = filled[o]
        filled[o] = k + 1
        index[2 * o + k] = t
        meta[o, pl.ds(k, 1), :] = by_tile[pl.ds(t, 1), :] * weight[t]
        meta[o, pl.ds(2 + k, 1), :] = jnp.full((1, TS), cell[t].astype(F32))


def place(x, y, z, c):
    return (lax.rem(y, NX) * 2 + c, lax.rem(x, NX) * NZ + lax.rem(z, NZ))


def main_kernel(
    index,
    shift,
    taps,
    weight,
    meta,
    b_rows,
    b_cols,
    raw,
    template,
    out,
    rawpad,
    snd,
    rcv,
    ysnd,
    yrcv,
    zrcv,
    wrcv,
    vsnd,
    vrcv,
    fin0,
    fin1,
    halo,
    ext,
    shifted,
    middle,
    conv,
    raw_sem,
    ext_sem,
    halo_ss,
    halo_rs,
    x_ss,
    x_rs,
    y_ss,
    y_rs,
    z_ss,
    z_rs,
    w_ss,
    w_rs,
    v_ss,
    v_rs,
    f_ss,
    f_rs,
):
    visit = lax.axis_index("visit")
    sky = lax.axis_index("sky")
    y, c = visit // 2, visit % 2
    x, z = sky // NZ, sky % NZ
    pos = jnp.where(c == 0, y, x)

    def along(step):
        return place(
            jnp.where(c == 0, x, x + step), jnp.where(c == 0, y + step, y), z, c
        )

    def remote(src, dst, ss, rs, to):
        return pltpu.make_async_remote_copy(
            src_ref=src, dst_ref=dst, send_sem=ss, recv_sem=rs, device_id=to, device_id_type=MESH
        )

    raw_copy = pltpu.make_async_copy(raw, rawpad.at[:, pl.ds(8, TS), :], raw_sem)
    raw_copy.start()

    def ext_copy(k):
        block = lax.rem(visit + 7 + k, 8)
        return pltpu.make_async_copy(
            template.at[:, pl.ds(pl.multiple_of(block * TS, TS), TS)],
            ext.at[pl.ds(16, 256), pl.ds(k * TS, TS)],
            ext_sem.at[k],
        )

    for k in range(3):
        ext_copy(k).start()

    barrier = pltpu.get_barrier_semaphore()
    up, down = lax.rem(sky + 1, OWNERS), lax.rem(sky + OWNERS - 1, OWNERS)
    greeted = [(visit, up), (visit, down), place(x, y, z + 1, c), place(x, y, z + NZ - 1, c), place(x, y, z, 1 - c)]
    for a in range(1, NX):
        for d in range(2):
            greeted += [place(x + a, y, z, d), place(x, y + a, z, d)]
    for to in greeted:
        pl.semaphore_signal(barrier, inc=1, device_id=to, device_id_type=MESH)

    @pl.when(x != y)
    def _():
        for d in range(2):
            pl.semaphore_signal(barrier, inc=1, device_id=place(y, x, z, d), device_id_type=MESH)

    blank = jnp.zeros((COUNT, 8, TS), F32)
    rawpad[:, 0:8, :] = blank
    rawpad[:, TS + 8 : TS + 16, :] = blank

    pl.semaphore_wait(barrier, len(greeted) + jnp.where(x != y, 2, 0))

    halo_up = remote(template.at[pl.ds(240, 16), :], halo.at[0], halo_ss.at[0], halo_rs.at[0], (visit, up))
    halo_down = remote(template.at[pl.ds(0, 16), :], halo.at[1], halo_ss.at[1], halo_rs.at[1], (visit, down))
    halo_up.start()
    halo_down.start()
    raw_copy.wait()

    lane = lax.broadcasted_iota(jnp.int32, (1, TS), 1)

    def warp(slot):
        found = index[slot]
        t = jnp.maximum(found, 0)
        w = jnp.where(found >= 0, weight[t], 0.0)
        rows = None
        for a in range(4):
            part = rawpad[t, pl.ds(shift[0, t] + (7 + a), TS), :] * (taps[0, a, t] * w)
            rows = part if rows is None else rows + part
        total = None
        for a in range(4):
            d = shift[1, t] + (a - 1)
            factor = jnp.where(jnp.logical_and(lane + d >= 0, lane + d < TS), taps[1, a, t], 0.0)
            part = pltpu.roll(rows, lax.rem(TS - d, TS), 1) * factor
            total = part if total is None else total + part
        return total

    def x_target(m):
        a, d = m // 2, m % 2
        return place(jnp.where(d == 0, x + a, x), jnp.where(d == 0, y, y + a), z, d)

    def x_copy(j, m):
        slot = m // 2 * 2 + c
        return remote(snd.at[j, m], rcv.at[j, slot], x_ss.at[j, m], x_rs.at[j, slot], x_target(m))

    def own_copy(j):
        return pltpu.make_async_copy(snd.at[j, c], rcv.at[j, c], x_rs.at[j, c])

    def send_tiles(j, first=0, end=8):
        @pl.loop(first, end)
        def _(i):
            a, d = jnp.where(i < 4, i // 2 * 2 + 1, 6 - i // 2 * 2), i % 2
            m = 2 * a + d
            owner_x = lax.rem(jnp.where(d == 0, x, y) + a, NX)
            owner_z = lax.rem(jnp.where(d == 0, z + 8 - j, z + 9 + j), NZ)
            owner = owner_x * NZ + owner_z
            for k in range(2):
                snd[j, m, k * TS : (k + 1) * TS, :] = warp(2 * owner + k)
            snd[j, m, 2 * TS : MSG, :] = meta[owner]

            @pl.when(m == c)
            def _():
                own_copy(j).start()

            @pl.when(m != c)
            def _():
                x_copy(j, m).start()

    def wait_tiles(j):
        @pl.loop(0, 8)
        def _(m):
            @pl.when(m == c)
            def _():
                own_copy(j).wait()

            @pl.when(m != c)
            def _():
                remote(snd.at[j, m], rcv.at[j, m], x_ss.at[j, m], x_rs.at[j, m], x_target(m)).wait_recv()

    sub = lax.broadcasted_iota(jnp.int32, (8, TS), 0)

    def gather_cells(j, h):
        for r in range(2):
            group = lax.rem(pos + (3 - h if r == 0 else 1 + h), NX)
            for e in range(2):
                cell = (r * 8 + group * 2 + e).astype(F32)
                pixels, row = None, None
                for m in range(8):
                    for k in range(2):
                        named = rcv[j, m, 2 * TS + 2 + k : 2 * TS + 3 + k, :]
                        mask = jnp.where(named == cell, 1.0, 0.0)
                        part = rcv[j, m, k * TS : (k + 1) * TS, :] * mask
                        pixels = part if pixels is None else pixels + part
                        part = rcv[j, m, 2 * TS + k : 2 * TS + 1 + k, :] * mask
                        row = part if row is None else row + part
                ysnd[j, h, e, r, 0:TS, :] = pixels
                ysnd[j, h, e, r, TS:CELL, :] = jnp.where(sub == 0, row, 0.0)

    def y_copy(j, h, r):
        to = along(1 if r == 0 else NX - 1)
        return remote(ysnd.at[j, h, 0, r], yrcv.at[j, h, r], y_ss.at[j, h, r], y_rs.at[j, h, r], to)

    def y_send(j, h):
        for r in range(2):
            y_copy(j, h, r).start()

    def y_take(j, h):
        for r in range(2):
            y_copy(j, h - 1, r).wait_recv()
            ysnd[j, h, 0, r] = ysnd[j, h, 0, r] + yrcv[j, h - 1, r]

    onward = place(x, y, jnp.where(c == 0, z + 1, z + NZ - 1), c)

    def z_copy(j):
        return remote(ysnd.at[j, 3, 0], zrcv.at[j], z_ss.at[j], z_rs.at[j], onward)

    def finish(j):
        y_take(j, 3)

        @pl.when(j >= 1)
        def _():
            z_copy(j - 1).wait_recv()
            ysnd[j, 3, 0] = ysnd[j, 3, 0] + zrcv[j - 1]

        @pl.when(jnp.logical_or(c == 0, j < STEPS - 1))
        def _():
            z_copy(j).start()

    def w_copy(j, h):
        return remote(ysnd.at[j, h, 1], wrcv.at[j, h], w_ss.at[j, h], w_rs.at[j, h], onward)

    def carry(j):
        @pl.loop(0, 4)
        def _(h):
            @pl.when(j >= 1)
            def _():
                w_copy(j - 1, h).wait_recv()
                ysnd[j, h, 1] = ysnd[j, h, 1] + wrcv[j - 1, h]

            @pl.when(jnp.logical_or(c == 0, j < STEPS - 1))
            def _():
                w_copy(j, h).start()

    def v_copy(h, r):
        to = along(1 if r == 0 else NX - 1)
        return remote(vsnd.at[h, r], vrcv.at[h, r], v_ss.at[h, r], v_rs.at[h, r], to)

    def v_step(h):
        @pl.when(c == 0)
        def _():
            w_copy(STEPS - 1, h).wait_recv()
            vsnd[h] = wrcv[STEPS - 1, h]

        @pl.when(c == 1)
        def _():
            vsnd[h] = ysnd[STEPS - 1, h, 1]

        for r in range(2):
            if h >= 1:
                v_copy(h - 1, r).wait_recv()
                vsnd[h, r] = vsnd[h, r] + vrcv[h - 1, r]
            if h < 3:
                v_copy(h, r).start()

    send_tiles(0)
    send_tiles(1)

    halo_up.wait_recv()
    halo_down.wait_recv()
    for k in range(3):
        ext_copy(k).wait()
    keep_up = jnp.where(sky > 0, 1.0, 0.0)
    keep_down = jnp.where(sky < OWNERS - 1, 1.0, 0.0)
    for k in range(3):
        block = pl.multiple_of(lax.rem(visit + 7 + k, 8) * TS, TS)
        cols = slice(k * TS, (k + 1) * TS)
        ext[0:16, cols] = halo[0, :, pl.ds(block, TS)] * keep_up
        ext[272:EXT, cols] = halo[1, :, pl.ds(block, TS)] * keep_down
    ext[:, 0:TS] = ext[:, 0:TS] * jnp.where(visit > 0, 1.0, 0.0)
    ext[:, 2 * TS :] = ext[:, 2 * TS :] * jnp.where(visit < 7, 1.0, 0.0)
    for v in range(KS):
        shifted[v] = ext[:, TS - 15 + v : 2 * TS - 15 + v]

    def convolve(b):
        total = shifted[0] * b_cols[b, 0]
        for v in range(1, KS):
            total = total + shifted[v] * b_cols[b, v]
        middle[...] = total
        total = middle[1:257, :] * b_rows[b, 0]
        for u in range(1, KS):
            total = total + middle[u + 1 : u + 257, :] * b_rows[b, u]
        conv[b] = total

    convolve(STEPS)

    @pl.loop(0, STEPS)
    def _(j):
        wait_tiles(j)
        gather_cells(j, 0)
        y_send(j, 0)
        for h in range(1, 3):

            @pl.when(j >= h)
            def _():
                y_take(j - h, h)
                y_send(j - h, h)

        @pl.when(j >= 3)
        def _():
            finish(j - 3)

        @pl.loop(1, 4)
        def _(h):
            gather_cells(j, h)

        carry(j)

        @pl.when(j + 2 < STEPS)
        def _():
            send_tiles(j + 2)

        convolve(j)

    last = STEPS - 1
    to_sibling = remote(vsnd.at[3], fin0, f_ss.at[0], f_rs.at[0], place(x, y, z, 1))
    to_even = remote(ysnd.at[last, 3, 0], fin1, f_ss.at[1], f_rs.at[1], place(y, x, z, 0))
    to_odd = remote(vsnd.at[3], fin1, f_ss.at[2], f_rs.at[1], place(y, x, z, 1))
    stay_odd = pltpu.make_async_copy(vsnd.at[3], fin1, f_rs.at[1])

    y_take(last, 1)
    y_send(last, 1)
    y_take(last - 1, 2)
    y_send(last - 1, 2)
    finish(last - 2)
    v_step(0)
    y_take(last, 2)
    y_send(last, 2)
    v_step(1)
    finish(last - 1)
    v_step(2)
    finish(last)

    @pl.when(c == 1)
    def _():
        to_even.start()

    v_step(3)

    @pl.when(c == 0)
    def _():
        to_sibling.start()
        z_copy(last).wait_recv()
        fin0[...] = zrcv[last]

    @pl.when(c == 1)
    def _():
        @pl.when(x != y)
        def _():
            to_odd.start()

        @pl.when(x == y)
        def _():
            stay_odd.start()

        to_sibling.wait_recv()

    @pl.when(jnp.logical_and(c == 1, x == y))
    def _():
        stay_odd.wait()

    @pl.when(jnp.logical_not(jnp.logical_and(c == 1, x == y)))
    def _():
        to_odd.wait_recv()

    xs = (2.0 * lane.astype(F32) + 1.0) / TS - 1.0
    ys = (2.0 * lax.broadcasted_iota(jnp.int32, (TS, 1), 0).astype(F32) + 1.0) / TS - 1.0
    ys = jnp.broadcast_to(ys, (TS, TS))
    for r in range(2):
        rows = slice(r * TS, (r + 1) * TS)
        coef = fin0[r, TS : TS + 1, :] + fin1[r, TS : TS + 1, :]
        total = fin0[r, 0:TS, :] + fin1[r, 0:TS, :]
        for b in range(NB):
            flat = coef[:, 3 * b : 3 * b + 1] + coef[:, 3 * b + 1 : 3 * b + 2] * xs
            field = flat + coef[:, 3 * b + 2 : 3 * b + 3] * ys
            total = total - conv[b, rows, :] * field
        out[rows, :] = total

    halo_up.wait_send()
    halo_down.wait_send()

    @pl.loop(0, STEPS)
    def _(j):
        @pl.loop(0, 8)
        def _(m):
            @pl.when(m != c)
            def _():
                x_copy(j, m).wait_send()

        for h in range(3):
            for r in range(2):
                y_copy(j, h, r).wait_send()

        @pl.when(jnp.logical_or(c == 0, j < STEPS - 1))
        def _():
            z_copy(j).wait_send()
            for h in range(4):
                w_copy(j, h).wait_send()

    for h in range(3):
        for r in range(2):
            v_copy(h, r).wait_send()

    @pl.when(c == 0)
    def _():
        to_sibling.wait_send()

    @pl.when(c == 1)
    def _():
        to_even.wait_send()

        @pl.when(x != y)
        def _():
            to_odd.wait_send()


def body(
    raw_tiles,
    warp_shift,
    warp_taps,
    match_coeffs,
    tile_weights,
    dest_owner,
    dest_cell,
    template,
    basis_rows,
    basis_cols,
):
    smem = pl.BlockSpec(memory_space=pltpu.SMEM)
    vmem = pl.BlockSpec(memory_space=pltpu.VMEM)
    hbm = pl.BlockSpec(memory_space=pl.ANY)
    index, meta = pl.pallas_call(
        tables_kernel,
        out_shape=(
            jax.ShapeDtypeStruct((2 * OWNERS,), jnp.int32),
            jax.ShapeDtypeStruct((OWNERS, 8, TS), F32),
        ),
        in_specs=[smem, smem, smem, vmem],
        out_specs=(smem, vmem),
        scratch_shapes=[
            pltpu.SMEM((OWNERS,), jnp.int32),
            pltpu.VMEM((TS, TS), F32),
            pltpu.VMEM((TS, TS), F32),
        ],
        name="tables",
    )(dest_owner.T, dest_cell, tile_weights, match_coeffs.T)
    dma = pltpu.SemaphoreType.DMA
    return pl.pallas_call(
        main_kernel,
        out_shape=jax.ShapeDtypeStruct((2 * TS, TS), F32),
        in_specs=[smem, smem, smem, smem, vmem, smem, smem, hbm, hbm],
        out_specs=vmem,
        scratch_shapes=[
            pltpu.VMEM((COUNT, TS + 16, TS), F32),
            pltpu.VMEM((STEPS, 8, MSG, TS), F32),
            pltpu.VMEM((STEPS, 8, MSG, TS), F32),
            pltpu.VMEM((STEPS, 4, 2, 2, CELL, TS), F32),
            pltpu.VMEM((STEPS, 3, 2, CELL, TS), F32),
            pltpu.VMEM((STEPS, 2, CELL, TS), F32),
            pltpu.VMEM((STEPS, 4, 2, CELL, TS), F32),
            pltpu.VMEM((4, 2, CELL, TS), F32),
            pltpu.VMEM((3, 2, CELL, TS), F32),
            pltpu.VMEM((2, CELL, TS), F32),
            pltpu.VMEM((2, CELL, TS), F32),
            pltpu.VMEM((2, 16, 8 * TS), F32),
            pltpu.VMEM((EXT, 3 * TS), F32),
            pltpu.VMEM((KS, EXT, TS), F32),
            pltpu.VMEM((EXT, TS), F32),
            pltpu.VMEM((NB, 2 * TS, TS), F32),
            dma,
            dma((3,)),
            dma((2,)),
            dma((2,)),
            dma((STEPS, 8)),
            dma((STEPS, 8)),
            dma((STEPS, 3, 2)),
            dma((STEPS, 3, 2)),
            dma((STEPS,)),
            dma((STEPS,)),
            dma((STEPS, 4)),
            dma((STEPS, 4)),
            dma((3, 2)),
            dma((3, 2)),
            dma((3,)),
            dma((2,)),
        ],
        compiler_params=pltpu.CompilerParams(
            collective_id=0, has_side_effects=True, vmem_limit_bytes=58 * 2**20
        ),
        name="exchange",
    )(
        index,
        warp_shift.T,
        jnp.transpose(warp_taps, (1, 2, 0)),
        tile_weights,
        meta,
        basis_rows,
        basis_cols,
        raw_tiles,
        template,
    )


def solution(mesh):
    return jax.shard_map(
        body,
        mesh=mesh,
        in_specs=(
            P(("visit", "sky"), None, None),
            P(("visit", "sky"), None),
            P(("visit", "sky"), None, None),
            P(("visit", "sky"), None),
            P(("visit", "sky")),
            P(("visit", "sky"), None),
            P(("visit", "sky")),
            P("sky", None),
            P(),
            P(),
        ),
        out_specs=P("sky", "visit"),
        check_vma=False,
    )
```

```python
import jax
import jax.numpy as jnp
from jax import lax
from jax.experimental import pallas as pl
from jax.experimental.pallas import tpu as pltpu
from jax.sharding import PartitionSpec as P

MESH = pl.DeviceIdType.MESH
F32 = jnp.float32
TS = 128
COUNT = 56
OWNERS = 64
NB = 9
KS = 31
NX = 4
NZ = 16
STEPS = 8
MSG = 2 * TS + 8
CELL = TS + 8
EXT = 288


def tables_kernel(
    owner_hbm, cell_hbm, weight_hbm, coef_hbm, index, meta, owner, cell, weight, coef, filled, square, by_tile, in_sem
):
    small = [(owner_hbm, owner), (cell_hbm, cell), (weight_hbm, weight), (coef_hbm, coef)]
    small = [pltpu.make_async_copy(src, dst, in_sem.at[i]) for i, (src, dst) in enumerate(small)]
    for copy in small:
        copy.start()
    meta[...] = jnp.zeros(meta.shape, F32)
    square[...] = jnp.zeros(square.shape, F32)

    @pl.loop(0, OWNERS)
    def _(o):
        filled[o] = 0
        index[2 * o] = -1
        index[2 * o + 1] = -1

    for copy in small:
        copy.wait()
    square[0 : 3 * NB, 0:COUNT] = coef[...]
    by_tile[...] = square[...].T

    @pl.loop(0, COUNT)
    def _(t):
        o = owner[0, t]
        k = filled[o]
        filled[o] = k + 1
        index[2 * o + k] = t
        meta[o, pl.ds(k, 1), :] = by_tile[pl.ds(t, 1), :] * weight[t]
        meta[o, pl.ds(2 + k, 1), :] = jnp.full((1, TS), cell[t].astype(F32))


def place(x, y, z, c):
    return (lax.rem(y, NX) * 2 + c, lax.rem(x, NX) * NZ + lax.rem(z, NZ))


def main_kernel(
    index_hbm,
    shift_hbm,
    taps_hbm,
    weight_hbm,
    meta_hbm,
    b_rows_hbm,
    b_cols_hbm,
    raw,
    template,
    out,
    index,
    shift,
    taps,
    weight,
    meta,
    b_rows,
    b_cols,
    rawpad,
    snd,
    rcv,
    ysnd,
    yrcv,
    zrcv,
    wrcv,
    vrcv,
    fin0,
    fin1,
    halo,
    ext,
    shifted,
    middle,
    conv,
    in_sem,
    raw_sem,
    ext_sem,
    halo_ss,
    halo_rs,
    x_ss,
    x_rs,
    y_ss,
    y_rs,
    z_ss,
    z_rs,
    w_ss,
    w_rs,
    v_ss,
    v_rs,
    f_ss,
    f_rs,
):
    visit = lax.axis_index("visit")
    sky = lax.axis_index("sky")
    y, c = visit // 2, visit % 2
    x, z = sky // NZ, sky % NZ
    pos = jnp.where(c == 0, y, x)

    def along(step):
        return place(
            jnp.where(c == 0, x, x + step), jnp.where(c == 0, y + step, y), z, c
        )

    def remote(src, dst, ss, rs, to):
        return pltpu.make_async_remote_copy(
            src_ref=src, dst_ref=dst, send_sem=ss, recv_sem=rs, device_id=to, device_id_type=MESH
        )

    small = [(index_hbm, index), (shift_hbm, shift), (taps_hbm, taps), (weight_hbm, weight), (meta_hbm, meta)]
    small += [(b_rows_hbm, b_rows), (b_cols_hbm, b_cols)]
    small = [pltpu.make_async_copy(src, dst, in_sem.at[i]) for i, (src, dst) in enumerate(small)]
    for copy in small:
        copy.start()
    raw_copy = pltpu.make_async_copy(raw, rawpad.at[:, pl.ds(8, TS), :], raw_sem)
    raw_copy.start()

    def ext_copy(k):
        block = lax.rem(visit + 7 + k, 8)
        return pltpu.make_async_copy(
            template.at[:, pl.ds(pl.multiple_of(block * TS, TS), TS)],
            ext.at[pl.ds(16, 256), pl.ds(k * TS, TS)],
            ext_sem.at[k],
        )

    for k in range(3):
        ext_copy(k).start()

    barrier = pltpu.get_barrier_semaphore()
    up, down = lax.rem(sky + 1, OWNERS), lax.rem(sky + OWNERS - 1, OWNERS)
    greeted = [(visit, up), (visit, down), place(x, y, z, 1 - c)]
    for d in range(2):
        greeted += [place(x, y, z + 1, d), place(x, y, z + NZ - 1, d)]
    for a in range(1, NX):
        for d in range(2):
            greeted += [place(x + a, y, z, d), place(x, y + a, z, d)]
    for to in greeted:
        pl.semaphore_signal(barrier, inc=1, device_id=to, device_id_type=MESH)

    @pl.when(x != y)
    def _():
        for d in range(2):
            pl.semaphore_signal(barrier, inc=1, device_id=place(y, x, z, d), device_id_type=MESH)

    blank = jnp.zeros((COUNT, 8, TS), F32)
    rawpad[:, 0:8, :] = blank
    rawpad[:, TS + 8 : TS + 16, :] = blank

    pl.semaphore_wait(barrier, len(greeted) + jnp.where(x != y, 2, 0))

    halo_up = remote(template.at[pl.ds(240, 16), :], halo.at[0], halo_ss.at[0], halo_rs.at[0], (visit, up))
    halo_down = remote(template.at[pl.ds(0, 16), :], halo.at[1], halo_ss.at[1], halo_rs.at[1], (visit, down))
    halo_up.start()
    halo_down.start()
    raw_copy.wait()
    for copy in small:
        copy.wait()

    lane = lax.broadcasted_iota(jnp.int32, (1, TS), 1)

    def warp(slot):
        found = index[slot]
        t = jnp.maximum(found, 0)
        w = jnp.where(found >= 0, weight[t], 0.0)
        rows = None
        for a in range(4):
            part = rawpad[t, pl.ds(shift[0, t] + (7 + a), TS), :] * (taps[0, a, t] * w)
            rows = part if rows is None else rows + part
        total = None
        for a in range(4):
            d = shift[1, t] + (a - 1)
            factor = jnp.where(jnp.logical_and(lane + d >= 0, lane + d < TS), taps[1, a, t], 0.0)
            part = pltpu.roll(rows, lax.rem(TS - d, TS), 1) * factor
            total = part if total is None else total + part
        return total

    def x_target(m):
        a, d = m // 2, m % 2
        return place(jnp.where(d == 0, x + a, x), jnp.where(d == 0, y, y + a), z, d)

    def x_copy(j, m):
        slot = m // 2 * 2 + c
        return remote(snd.at[j, m], rcv.at[j, slot], x_ss.at[j, m], x_rs.at[j, slot], x_target(m))

    def own_copy(j):
        return pltpu.make_async_copy(snd.at[j, c], rcv.at[j, c], x_rs.at[j, c])

    def send_tiles(j, first=0, end=8):
        @pl.loop(first, end)
        def _(i):
            a, d = jnp.where(i < 4, i // 2 * 2 + 1, 6 - i // 2 * 2), i % 2
            m = 2 * a + d
            owner_x = lax.rem(jnp.where(d == 0, x, y) + a, NX)
            owner_z = lax.rem(jnp.where(d == 0, z + 8 - j, z + 9 + j), NZ)
            owner = owner_x * NZ + owner_z
            for k in range(2):
                snd[j, m, k * TS : (k + 1) * TS, :] = warp(2 * owner + k)
            snd[j, m, 2 * TS : MSG, :] = meta[owner]

            @pl.when(m == c)
            def _():
                own_copy(j).start()

            @pl.when(m != c)
            def _():
                x_copy(j, m).start()

    def wait_tiles(j):
        @pl.loop(0, 8)
        def _(m):
            @pl.when(m == c)
            def _():
                own_copy(j).wait()

            @pl.when(m != c)
            def _():
                remote(snd.at[j, m], rcv.at[j, m], x_ss.at[j, m], x_rs.at[j, m], x_target(m)).wait_recv()

    sub = lax.broadcasted_iota(jnp.int32, (8, TS), 0)

    def gather_cells(j, h):
        for r in range(2):
            group = lax.rem(pos + (3 - h if r == 0 else 1 + h), NX)
            for e in range(2):
                cell = (r * 8 + group * 2 + e).astype(F32)
                pixels, row = None, None
                for m in range(8):
                    for k in range(2):
                        named = rcv[j, m, 2 * TS + 2 + k : 2 * TS + 3 + k, :]
                        mask = jnp.where(named == cell, 1.0, 0.0)
                        part = rcv[j, m, k * TS : (k + 1) * TS, :] * mask
                        pixels = part if pixels is None else pixels + part
                        part = rcv[j, m, 2 * TS + k : 2 * TS + 1 + k, :] * mask
                        row = part if row is None else row + part
                ysnd[j, h, e, r, 0:TS, :] = pixels
                ysnd[j, h, e, r, TS:CELL, :] = jnp.where(sub == 0, row, 0.0)

    def y_copy(j, h, r):
        to = along(1 if r == 0 else NX - 1)
        return remote(ysnd.at[j, h, 0, r], yrcv.at[j, h, r], y_ss.at[j, h, r], y_rs.at[j, h, r], to)

    def y_send(j, h):
        for r in range(2):
            y_copy(j, h, r).start()

    def y_take(j, h):
        for r in range(2):
            y_copy(j, h - 1, r).wait_recv()
            ysnd[j, h, 0, r] = ysnd[j, h, 0, r] + yrcv[j, h - 1, r]

    onward = place(x, y, jnp.where(c == 0, z + 1, z + NZ - 1), c)

    def z_copy(j):
        return remote(ysnd.at[j, 3, 0], zrcv.at[j], z_ss.at[j], z_rs.at[j], onward)

    def finish(j):
        y_take(j, 3)

        @pl.when(j >= 1)
        def _():
            z_copy(j - 1).wait_recv()
            ysnd[j, 3, 0] = ysnd[j, 3, 0] + zrcv[j - 1]

        @pl.when(jnp.logical_or(c == 0, j < STEPS - 1))
        def _():
            z_copy(j).start()

    def w_copy(j, h):
        return remote(ysnd.at[j, h, 1], wrcv.at[j, h], w_ss.at[j, h], w_rs.at[j, h], onward)

    def carry(j):
        @pl.loop(0, 4)
        def _(h):
            @pl.when(j >= 1)
            def _():
                w_copy(j - 1, h).wait_recv()
                ysnd[j, h, 1] = ysnd[j, h, 1] + wrcv[j - 1, h]

            @pl.when(j < STEPS - 1)
            def _():
                w_copy(j, h).start()

    def v_copy(h, r):
        to = along(1 if r == 0 else NX - 1)
        return remote(ysnd.at[last, h, 1, r], vrcv.at[h, r], v_ss.at[h, r], v_rs.at[h, r], to)

    def v_step(h):
        for r in range(2):
            if h >= 1:
                v_copy(h - 1, r).wait_recv()
                ysnd[last, h, 1, r] = ysnd[last, h, 1, r] + vrcv[h - 1, r]
            if h < 3:
                v_copy(h, r).start()

    last = STEPS - 1
    def sent(j):
        @pl.loop(0, 8)
        def _(m):
            @pl.when(m != c)
            def _():
                x_copy(j, m).wait_send()

        for h in range(3):
            for r in range(2):
                y_copy(j, h, r).wait_send()

        @pl.when(jnp.logical_or(c == 0, j < STEPS - 1))
        def _():
            z_copy(j).wait_send()

        @pl.when(j < STEPS - 1)
        def _():
            for h in range(4):
                w_copy(j, h).wait_send()

    send_tiles(0)
    send_tiles(1)

    halo_up.wait_recv()
    halo_down.wait_recv()
    for k in range(3):
        ext_copy(k).wait()
    keep_up = jnp.where(sky > 0, 1.0, 0.0)
    keep_down = jnp.where(sky < OWNERS - 1, 1.0, 0.0)
    for k in range(3):
        block = pl.multiple_of(lax.rem(visit + 7 + k, 8) * TS, TS)
        cols = slice(k * TS, (k + 1) * TS)
        ext[0:16, cols] = halo[0, :, pl.ds(block, TS)] * keep_up
        ext[272:EXT, cols] = halo[1, :, pl.ds(block, TS)] * keep_down
    ext[:, 0:TS] = ext[:, 0:TS] * jnp.where(visit > 0, 1.0, 0.0)
    ext[:, 2 * TS :] = ext[:, 2 * TS :] * jnp.where(visit < 7, 1.0, 0.0)
    for v in range(KS):
        shifted[v] = ext[:, TS - 15 + v : 2 * TS - 15 + v]

    def convolve(b):
        total = shifted[0] * b_cols[b, 0]
        for v in range(1, KS):
            total = total + shifted[v] * b_cols[b, v]
        middle[...] = total
        total = middle[1:257, :] * b_rows[b, 0]
        for u in range(1, KS):
            total = total + middle[u + 1 : u + 257, :] * b_rows[b, u]
        conv[b] = total

    convolve(STEPS - 1)
    convolve(STEPS)

    @pl.loop(0, STEPS)
    def _(j):
        wait_tiles(j)
        gather_cells(j, 0)
        y_send(j, 0)
        for h in range(1, 3):

            @pl.when(j >= h)
            def _():
                y_take(j - h, h)
                y_send(j - h, h)

        @pl.when(j >= 3)
        def _():
            finish(j - 3)

        @pl.loop(1, 4)
        def _(h):
            gather_cells(j, h)

        carry(j)

        @pl.when(j + 2 < STEPS)
        def _():
            send_tiles(j + 2)

        @pl.when(j >= 4)
        def _():
            sent(j - 4)

        @pl.when(j < STEPS - 1)
        def _():
            convolve(j)

    to_next = remote(ysnd.at[last, 3, 1], fin0, f_ss.at[0], f_rs.at[0], place(x, y, z + 1, 1))
    to_even = remote(ysnd.at[last, 3, 0], fin1, f_ss.at[1], f_rs.at[1], place(y, x, z, 0))
    to_odd = remote(ysnd.at[last, 3, 1], fin1, f_ss.at[2], f_rs.at[1], place(y, x, z, 1))
    stay_odd = pltpu.make_async_copy(ysnd.at[last, 3, 1], fin1, f_rs.at[1])

    v_step(0)
    y_take(last, 1)
    y_send(last, 1)
    y_take(last - 1, 2)
    y_send(last - 1, 2)
    finish(last - 2)
    v_step(1)
    y_take(last, 2)
    y_send(last, 2)
    v_step(2)
    finish(last - 1)
    finish(last)

    @pl.when(c == 1)
    def _():
        to_even.start()

    v_step(3)

    @pl.when(c == 0)
    def _():
        to_next.start()
        z_copy(last).wait_recv()
        fin0[...] = zrcv[last]

    @pl.when(c == 1)
    def _():
        @pl.when(x != y)
        def _():
            to_odd.start()

        @pl.when(x == y)
        def _():
            stay_odd.start()

        to_next.wait_recv()

    @pl.when(jnp.logical_and(c == 1, x == y))
    def _():
        stay_odd.wait()

    @pl.when(jnp.logical_not(jnp.logical_and(c == 1, x == y)))
    def _():
        to_odd.wait_recv()

    xs = (2.0 * lane.astype(F32) + 1.0) / TS - 1.0
    ys = (2.0 * lax.broadcasted_iota(jnp.int32, (TS, 1), 0).astype(F32) + 1.0) / TS - 1.0
    ys = jnp.broadcast_to(ys, (TS, TS))
    for r in range(2):
        rows = slice(r * TS, (r + 1) * TS)
        coef = fin0[r, TS : TS + 1, :] + fin1[r, TS : TS + 1, :]
        total = fin0[r, 0:TS, :] + fin1[r, 0:TS, :]
        for b in range(NB):
            flat = coef[:, 3 * b : 3 * b + 1] + coef[:, 3 * b + 1 : 3 * b + 2] * xs
            field = flat + coef[:, 3 * b + 2 : 3 * b + 3] * ys
            total = total - conv[b, rows, :] * field
        out[rows, :] = total

    halo_up.wait_send()
    halo_down.wait_send()

    @pl.loop(STEPS - 4, STEPS)
    def _(j):
        sent(j)

    for h in range(3):
        for r in range(2):
            v_copy(h, r).wait_send()

    @pl.when(c == 0)
    def _():
        to_next.wait_send()

    @pl.when(c == 1)
    def _():
        to_even.wait_send()

        @pl.when(x != y)
        def _():
            to_odd.wait_send()


def body(
    raw_tiles,
    warp_shift,
    warp_taps,
    match_coeffs,
    tile_weights,
    dest_owner,
    dest_cell,
    template,
    basis_rows,
    basis_cols,
):
    smem = pl.BlockSpec(memory_space=pltpu.SMEM)
    vmem = pl.BlockSpec(memory_space=pltpu.VMEM)
    hbm = pl.BlockSpec(memory_space=pl.ANY)
    index, meta = pl.pallas_call(
        tables_kernel,
        out_shape=(
            jax.ShapeDtypeStruct((2 * OWNERS,), jnp.int32),
            jax.ShapeDtypeStruct((OWNERS, 8, TS), F32),
        ),
        in_specs=[hbm] * 4,
        out_specs=(smem, vmem),
        scratch_shapes=[
            pltpu.SMEM((1, COUNT), jnp.int32),
            pltpu.SMEM((COUNT,), jnp.int32),
            pltpu.SMEM((COUNT,), F32),
            pltpu.VMEM((3 * NB, COUNT), F32),
            pltpu.SMEM((OWNERS,), jnp.int32),
            pltpu.VMEM((TS, TS), F32),
            pltpu.VMEM((TS, TS), F32),
            pltpu.SemaphoreType.DMA((4,)),
        ],
        name="tables",
    )(dest_owner.T, dest_cell, tile_weights, match_coeffs.T)
    dma = pltpu.SemaphoreType.DMA
    return pl.pallas_call(
        main_kernel,
        out_shape=jax.ShapeDtypeStruct((2 * TS, TS), F32),
        in_specs=[hbm] * 9,
        out_specs=vmem,
        scratch_shapes=[
            pltpu.SMEM((2 * OWNERS,), jnp.int32),
            pltpu.SMEM((2, COUNT), jnp.int32),
            pltpu.SMEM((2, 4, COUNT), F32),
            pltpu.SMEM((COUNT,), F32),
            pltpu.VMEM((OWNERS, 8, TS), F32),
            pltpu.SMEM((NB, KS), F32),
            pltpu.SMEM((NB, KS), F32),
            pltpu.VMEM((COUNT, TS + 16, TS), F32),
            pltpu.VMEM((STEPS, 8, MSG, TS), F32),
            pltpu.VMEM((STEPS, 8, MSG, TS), F32),
            pltpu.VMEM((STEPS, 4, 2, 2, CELL, TS), F32),
            pltpu.VMEM((STEPS, 3, 2, CELL, TS), F32),
            pltpu.VMEM((STEPS, 2, CELL, TS), F32),
            pltpu.VMEM((STEPS, 4, 2, CELL, TS), F32),
            pltpu.VMEM((3, 2, CELL, TS), F32),
            pltpu.VMEM((2, CELL, TS), F32),
            pltpu.VMEM((2, CELL, TS), F32),
            pltpu.VMEM((2, 16, 8 * TS), F32),
            pltpu.VMEM((EXT, 3 * TS), F32),
            pltpu.VMEM((KS, EXT, TS), F32),
            pltpu.VMEM((EXT, TS), F32),
            pltpu.VMEM((NB, 2 * TS, TS), F32),
            dma((7,)),
            dma,
            dma((3,)),
            dma((2,)),
            dma((2,)),
            dma((STEPS, 8)),
            dma((STEPS, 8)),
            dma((STEPS, 3, 2)),
            dma((STEPS, 3, 2)),
            dma((STEPS,)),
            dma((STEPS,)),
            dma((STEPS, 4)),
            dma((STEPS, 4)),
            dma((3, 2)),
            dma((3, 2)),
            dma((3,)),
            dma((2,)),
        ],
        compiler_params=pltpu.CompilerParams(
            collective_id=0, has_side_effects=True, vmem_limit_bytes=58 * 2**20
        ),
        name="exchange",
    )(
        index,
        warp_shift.T,
        jnp.transpose(warp_taps, (1, 2, 0)),
        tile_weights,
        meta,
        basis_rows,
        basis_cols,
        raw_tiles,
        template,
    )


def solution(mesh):
    return jax.shard_map(
        body,
        mesh=mesh,
        in_specs=(
            P(("visit", "sky"), None, None),
            P(("visit", "sky"), None),
            P(("visit", "sky"), None, None),
            P(("visit", "sky"), None),
            P(("visit", "sky")),
            P(("visit", "sky"), None),
            P(("visit", "sky")),
            P("sky", None),
            P(),
            P(),
        ),
        out_specs=P("sky", "visit"),
        check_vma=False,
    )
```

```python
import jax
import jax.numpy as jnp
from jax import lax
from jax.experimental import pallas as pl
from jax.experimental.pallas import tpu as pltpu
from jax.sharding import PartitionSpec as P

MESH = pl.DeviceIdType.MESH
F32 = jnp.float32
TS = 128
COUNT = 56
OWNERS = 64
NB = 9
KS = 31
NX = 4
NZ = 16
STEPS = 8
MSG = 2 * TS + 8
CELL = TS + 8
EXT = 288


def tables_kernel(
    owner_hbm, cell_hbm, weight_hbm, coef_hbm, index, meta, owner, cell, weight, coef, filled, square, by_tile, in_sem
):
    small = [(owner_hbm, owner), (cell_hbm, cell), (weight_hbm, weight), (coef_hbm, coef)]
    small = [pltpu.make_async_copy(src, dst, in_sem.at[i]) for i, (src, dst) in enumerate(small)]
    for copy in small:
        copy.start()
    meta[...] = jnp.zeros(meta.shape, F32)
    square[...] = jnp.zeros(square.shape, F32)

    @pl.loop(0, OWNERS)
    def _(o):
        filled[o] = 0
        index[2 * o] = -1
        index[2 * o + 1] = -1

    for copy in small:
        copy.wait()
    square[0 : 3 * NB, 0:COUNT] = coef[...]
    by_tile[...] = square[...].T

    @pl.loop(0, COUNT)
    def _(t):
        o = owner[0, t]
        k = filled[o]
        filled[o] = k + 1
        index[2 * o + k] = t
        meta[o, pl.ds(k, 1), :] = by_tile[pl.ds(t, 1), :] * weight[t]
        meta[o, pl.ds(2 + k, 1), :] = jnp.full((1, TS), cell[t].astype(F32))


def place(x, y, z, c):
    return (lax.rem(y, NX) * 2 + c, lax.rem(x, NX) * NZ + lax.rem(z, NZ))


def main_kernel(
    index_hbm,
    shift_hbm,
    taps_hbm,
    weight_hbm,
    meta_hbm,
    b_rows_hbm,
    b_cols_hbm,
    raw,
    template,
    out,
    index,
    shift,
    taps,
    weight,
    meta,
    b_rows,
    b_cols,
    rawpad,
    snd,
    rcv,
    ysnd,
    yrcv,
    zrcv,
    wrcv,
    vrcv,
    fin0,
    fin1,
    halo,
    ext,
    shifted,
    middle,
    conv,
    in_sem,
    raw_sem,
    ext_sem,
    halo_ss,
    halo_rs,
    x_ss,
    x_rs,
    y_ss,
    y_rs,
    z_ss,
    z_rs,
    w_ss,
    w_rs,
    v_ss,
    v_rs,
    f_ss,
    f_rs,
):
    visit = lax.axis_index("visit")
    sky = lax.axis_index("sky")
    y, c = visit // 2, visit % 2
    x, z = sky // NZ, sky % NZ
    pos = jnp.where(c == 0, y, x)

    def along(step):
        return place(
            jnp.where(c == 0, x, x + step), jnp.where(c == 0, y + step, y), z, c
        )

    def remote(src, dst, ss, rs, to):
        return pltpu.make_async_remote_copy(
            src_ref=src, dst_ref=dst, send_sem=ss, recv_sem=rs, device_id=to, device_id_type=MESH
        )

    barrier = pltpu.get_barrier_semaphore()
    up, down = lax.rem(sky + 1, OWNERS), lax.rem(sky + OWNERS - 1, OWNERS)
    greeted = [(visit, up), (visit, down), place(x, y, z, 1 - c)]
    for d in range(2):
        greeted += [place(x, y, z + 1, d), place(x, y, z + NZ - 1, d)]
    for a in range(1, NX):
        for d in range(2):
            greeted += [place(x + a, y, z, d), place(x, y + a, z, d)]
    for to in greeted:
        pl.semaphore_signal(barrier, inc=1, device_id=to, device_id_type=MESH)

    @pl.when(x != y)
    def _():
        for d in range(2):
            pl.semaphore_signal(barrier, inc=1, device_id=place(y, x, z, d), device_id_type=MESH)

    small = [(index_hbm, index), (shift_hbm, shift), (taps_hbm, taps), (weight_hbm, weight), (meta_hbm, meta)]
    small += [(b_rows_hbm, b_rows), (b_cols_hbm, b_cols)]
    small = [pltpu.make_async_copy(src, dst, in_sem.at[i]) for i, (src, dst) in enumerate(small)]
    for copy in small:
        copy.start()
    raw_copy = pltpu.make_async_copy(raw, rawpad.at[:, pl.ds(8, TS), :], raw_sem)
    raw_copy.start()

    def ext_copy(k):
        block = lax.rem(visit + 7 + k, 8)
        return pltpu.make_async_copy(
            template.at[:, pl.ds(pl.multiple_of(block * TS, TS), TS)],
            ext.at[pl.ds(16, 256), pl.ds(k * TS, TS)],
            ext_sem.at[k],
        )

    for k in range(3):
        ext_copy(k).start()

    blank = jnp.zeros((COUNT, 8, TS), F32)
    rawpad[:, 0:8, :] = blank
    rawpad[:, TS + 8 : TS + 16, :] = blank

    pl.semaphore_wait(barrier, len(greeted) + jnp.where(x != y, 2, 0))

    halo_up = remote(template.at[pl.ds(240, 16), :], halo.at[0], halo_ss.at[0], halo_rs.at[0], (visit, up))
    halo_down = remote(template.at[pl.ds(0, 16), :], halo.at[1], halo_ss.at[1], halo_rs.at[1], (visit, down))
    halo_up.start()
    halo_down.start()
    raw_copy.wait()
    for copy in small:
        copy.wait()

    lane = lax.broadcasted_iota(jnp.int32, (1, TS), 1)

    def warp(slot):
        found = index[slot]
        t = jnp.maximum(found, 0)
        w = jnp.where(found >= 0, weight[t], 0.0)
        rows = None
        for a in range(4):
            part = rawpad[t, pl.ds(shift[0, t] + (7 + a), TS), :] * (taps[0, a, t] * w)
            rows = part if rows is None else rows + part
        total = None
        for a in range(4):
            d = shift[1, t] + (a - 1)
            factor = jnp.where(jnp.logical_and(lane + d >= 0, lane + d < TS), taps[1, a, t], 0.0)
            part = pltpu.roll(rows, lax.rem(TS - d, TS), 1) * factor
            total = part if total is None else total + part
        return total

    def x_target(m):
        a, d = m // 2, m % 2
        return place(jnp.where(d == 0, x + a, x), jnp.where(d == 0, y, y + a), z, d)

    def x_copy(j, m):
        slot = m // 2 * 2 + c
        return remote(snd.at[j, m], rcv.at[j, slot], x_ss.at[j, m], x_rs.at[j, slot], x_target(m))

    def own_copy(j):
        return pltpu.make_async_copy(snd.at[j, c], rcv.at[j, c], x_rs.at[j, c])

    def send_tiles(j, first=0, end=8):
        @pl.loop(first, end)
        def _(i):
            a, d = jnp.where(i < 4, i // 2 * 2 + 1, 6 - i // 2 * 2), i % 2
            m = 2 * a + d
            owner_x = lax.rem(jnp.where(d == 0, x, y) + a, NX)
            owner_z = lax.rem(jnp.where(d == 0, z + 8 - j, z + 9 + j), NZ)
            owner = owner_x * NZ + owner_z
            for k in range(2):
                snd[j, m, k * TS : (k + 1) * TS, :] = warp(2 * owner + k)
            snd[j, m, 2 * TS : MSG, :] = meta[owner]

            @pl.when(m == c)
            def _():
                own_copy(j).start()

            @pl.when(m != c)
            def _():
                x_copy(j, m).start()

    def wait_tiles(j):
        @pl.loop(0, 8)
        def _(m):
            @pl.when(m == c)
            def _():
                own_copy(j).wait()

            @pl.when(m != c)
            def _():
                remote(snd.at[j, m], rcv.at[j, m], x_ss.at[j, m], x_rs.at[j, m], x_target(m)).wait_recv()

    sub = lax.broadcasted_iota(jnp.int32, (8, TS), 0)

    def gather_cells(j, h):
        for r in range(2):
            group = lax.rem(pos + (3 - h if r == 0 else 1 + h), NX)
            for e in range(2):
                cell = (r * 8 + group * 2 + e).astype(F32)
                pixels, row = None, None
                for m in range(8):
                    for k in range(2):
                        named = rcv[j, m, 2 * TS + 2 + k : 2 * TS + 3 + k, :]
                        mask = jnp.where(named == cell, 1.0, 0.0)
                        part = rcv[j, m, k * TS : (k + 1) * TS, :] * mask
                        pixels = part if pixels is None else pixels + part
                        part = rcv[j, m, 2 * TS + k : 2 * TS + 1 + k, :] * mask
                        row = part if row is None else row + part
                ysnd[j, h, e, r, 0:TS, :] = pixels
                ysnd[j, h, e, r, TS:CELL, :] = jnp.where(sub == 0, row, 0.0)

    def y_copy(j, h, r):
        to = along(1 if r == 0 else NX - 1)
        return remote(ysnd.at[j, h, 0, r], yrcv.at[j, h, r], y_ss.at[j, h, r], y_rs.at[j, h, r], to)

    def y_send(j, h):
        for r in range(2):
            y_copy(j, h, r).start()

    def y_take(j, h):
        for r in range(2):
            y_copy(j, h - 1, r).wait_recv()
            ysnd[j, h, 0, r] = ysnd[j, h, 0, r] + yrcv[j, h - 1, r]

    onward = place(x, y, jnp.where(c == 0, z + 1, z + NZ - 1), c)

    def z_copy(j):
        return remote(ysnd.at[j, 3, 0], zrcv.at[j], z_ss.at[j], z_rs.at[j], onward)

    def finish(j):
        y_take(j, 3)

        @pl.when(j >= 1)
        def _():
            z_copy(j - 1).wait_recv()
            ysnd[j, 3, 0] = ysnd[j, 3, 0] + zrcv[j - 1]

        @pl.when(jnp.logical_or(c == 0, j < STEPS - 1))
        def _():
            z_copy(j).start()

    def w_copy(j, h):
        return remote(ysnd.at[j, h, 1], wrcv.at[j, h], w_ss.at[j, h], w_rs.at[j, h], onward)

    def carry(j):
        @pl.loop(0, 4)
        def _(h):
            @pl.when(j >= 1)
            def _():
                w_copy(j - 1, h).wait_recv()
                ysnd[j, h, 1] = ysnd[j, h, 1] + wrcv[j - 1, h]

            @pl.when(j < STEPS - 1)
            def _():
                w_copy(j, h).start()

    def v_copy(h, r):
        to = along(1 if r == 0 else NX - 1)
        return remote(ysnd.at[last, h, 1, r], vrcv.at[h, r], v_ss.at[h, r], v_rs.at[h, r], to)

    def v_step(h):
        for r in range(2):
            if h >= 1:
                v_copy(h - 1, r).wait_recv()
                ysnd[last, h, 1, r] = ysnd[last, h, 1, r] + vrcv[h - 1, r]
            if h < 3:
                v_copy(h, r).start()

    last = STEPS - 1
    def sent(j):
        @pl.loop(0, 8)
        def _(m):
            @pl.when(m != c)
            def _():
                x_copy(j, m).wait_send()

        for h in range(3):
            for r in range(2):
                y_copy(j, h, r).wait_send()

        @pl.when(jnp.logical_or(c == 0, j < STEPS - 1))
        def _():
            z_copy(j).wait_send()

        @pl.when(j < STEPS - 1)
        def _():
            for h in range(4):
                w_copy(j, h).wait_send()

    send_tiles(0)
    send_tiles(1)

    halo_up.wait_recv()
    halo_down.wait_recv()
    for k in range(3):
        ext_copy(k).wait()
    keep_up = jnp.where(sky > 0, 1.0, 0.0)
    keep_down = jnp.where(sky < OWNERS - 1, 1.0, 0.0)
    for k in range(3):
        block = pl.multiple_of(lax.rem(visit + 7 + k, 8) * TS, TS)
        cols = slice(k * TS, (k + 1) * TS)
        ext[0:16, cols] = halo[0, :, pl.ds(block, TS)] * keep_up
        ext[272:EXT, cols] = halo[1, :, pl.ds(block, TS)] * keep_down
    ext[:, 0:TS] = ext[:, 0:TS] * jnp.where(visit > 0, 1.0, 0.0)
    ext[:, 2 * TS :] = ext[:, 2 * TS :] * jnp.where(visit < 7, 1.0, 0.0)
    for v in range(KS):
        shifted[v] = ext[:, TS - 15 + v : 2 * TS - 15 + v]

    def convolve(b):
        total = shifted[0] * b_cols[b, 0]
        for v in range(1, KS):
            total = total + shifted[v] * b_cols[b, v]
        middle[...] = total
        total = middle[1:257, :] * b_rows[b, 0]
        for u in range(1, KS):
            total = total + middle[u + 1 : u + 257, :] * b_rows[b, u]
        conv[b] = total

    convolve(STEPS - 1)
    convolve(STEPS)

    @pl.loop(0, STEPS)
    def _(j):
        wait_tiles(j)
        gather_cells(j, 0)
        y_send(j, 0)
        for h in range(1, 3):

            @pl.when(j >= h)
            def _():
                y_take(j - h, h)
                y_send(j - h, h)

        @pl.when(j >= 3)
        def _():
            finish(j - 3)

        @pl.loop(1, 4)
        def _(h):
            gather_cells(j, h)

        carry(j)

        @pl.when(j + 2 < STEPS)
        def _():
            send_tiles(j + 2)

        @pl.when(j >= 4)
        def _():
            sent(j - 4)

        @pl.when(j < STEPS - 1)
        def _():
            convolve(j)

    to_next = remote(ysnd.at[last, 3, 1], fin0, f_ss.at[0], f_rs.at[0], place(x, y, z + 1, 1))
    to_even = remote(ysnd.at[last, 3, 0], fin1, f_ss.at[1], f_rs.at[1], place(y, x, z, 0))
    to_odd = remote(ysnd.at[last, 3, 1], fin1, f_ss.at[2], f_rs.at[1], place(y, x, z, 1))
    stay_odd = pltpu.make_async_copy(ysnd.at[last, 3, 1], fin1, f_rs.at[1])

    v_step(0)
    y_take(last, 1)
    y_send(last, 1)
    y_take(last - 1, 2)
    y_send(last - 1, 2)
    finish(last - 2)
    v_step(1)
    y_take(last, 2)
    y_send(last, 2)
    v_step(2)
    finish(last - 1)
    finish(last)

    @pl.when(c == 1)
    def _():
        to_even.start()

    v_step(3)

    @pl.when(c == 0)
    def _():
        to_next.start()
        z_copy(last).wait_recv()
        fin0[...] = zrcv[last]

    @pl.when(c == 1)
    def _():
        @pl.when(x != y)
        def _():
            to_odd.start()

        @pl.when(x == y)
        def _():
            stay_odd.start()

        to_next.wait_recv()

    @pl.when(jnp.logical_and(c == 1, x == y))
    def _():
        stay_odd.wait()

    @pl.when(jnp.logical_not(jnp.logical_and(c == 1, x == y)))
    def _():
        to_odd.wait_recv()

    xs = (2.0 * lane.astype(F32) + 1.0) / TS - 1.0
    ys = (2.0 * lax.broadcasted_iota(jnp.int32, (TS, 1), 0).astype(F32) + 1.0) / TS - 1.0
    ys = jnp.broadcast_to(ys, (TS, TS))
    for r in range(2):
        rows = slice(r * TS, (r + 1) * TS)
        coef = fin0[r, TS : TS + 1, :] + fin1[r, TS : TS + 1, :]
        total = fin0[r, 0:TS, :] + fin1[r, 0:TS, :]
        for b in range(NB):
            flat = coef[:, 3 * b : 3 * b + 1] + coef[:, 3 * b + 1 : 3 * b + 2] * xs
            field = flat + coef[:, 3 * b + 2 : 3 * b + 3] * ys
            total = total - conv[b, rows, :] * field
        out[rows, :] = total

    halo_up.wait_send()
    halo_down.wait_send()

    @pl.loop(STEPS - 4, STEPS)
    def _(j):
        sent(j)

    for h in range(3):
        for r in range(2):
            v_copy(h, r).wait_send()

    @pl.when(c == 0)
    def _():
        to_next.wait_send()

    @pl.when(c == 1)
    def _():
        to_even.wait_send()

        @pl.when(x != y)
        def _():
            to_odd.wait_send()


def body(
    raw_tiles,
    warp_shift,
    warp_taps,
    match_coeffs,
    tile_weights,
    dest_owner,
    dest_cell,
    template,
    basis_rows,
    basis_cols,
):
    smem = pl.BlockSpec(memory_space=pltpu.SMEM)
    vmem = pl.BlockSpec(memory_space=pltpu.VMEM)
    hbm = pl.BlockSpec(memory_space=pl.ANY)
    index, meta = pl.pallas_call(
        tables_kernel,
        out_shape=(
            jax.ShapeDtypeStruct((2 * OWNERS,), jnp.int32),
            jax.ShapeDtypeStruct((OWNERS, 8, TS), F32),
        ),
        in_specs=[hbm] * 4,
        out_specs=(smem, vmem),
        scratch_shapes=[
            pltpu.SMEM((1, COUNT), jnp.int32),
            pltpu.SMEM((COUNT,), jnp.int32),
            pltpu.SMEM((COUNT,), F32),
            pltpu.VMEM((3 * NB, COUNT), F32),
            pltpu.SMEM((OWNERS,), jnp.int32),
            pltpu.VMEM((TS, TS), F32),
            pltpu.VMEM((TS, TS), F32),
            pltpu.SemaphoreType.DMA((4,)),
        ],
        name="tables",
    )(dest_owner.T, dest_cell, tile_weights, match_coeffs.T)
    dma = pltpu.SemaphoreType.DMA
    return pl.pallas_call(
        main_kernel,
        out_shape=jax.ShapeDtypeStruct((2 * TS, TS), F32),
        in_specs=[hbm] * 9,
        out_specs=vmem,
        scratch_shapes=[
            pltpu.SMEM((2 * OWNERS,), jnp.int32),
            pltpu.SMEM((2, COUNT), jnp.int32),
            pltpu.SMEM((2, 4, COUNT), F32),
            pltpu.SMEM((COUNT,), F32),
            pltpu.VMEM((OWNERS, 8, TS), F32),
            pltpu.SMEM((NB, KS), F32),
            pltpu.SMEM((NB, KS), F32),
            pltpu.VMEM((COUNT, TS + 16, TS), F32),
            pltpu.VMEM((STEPS, 8, MSG, TS), F32),
            pltpu.VMEM((STEPS, 8, MSG, TS), F32),
            pltpu.VMEM((STEPS, 4, 2, 2, CELL, TS), F32),
            pltpu.VMEM((STEPS, 3, 2, CELL, TS), F32),
            pltpu.VMEM((STEPS, 2, CELL, TS), F32),
            pltpu.VMEM((STEPS, 4, 2, CELL, TS), F32),
            pltpu.VMEM((3, 2, CELL, TS), F32),
            pltpu.VMEM((2, CELL, TS), F32),
            pltpu.VMEM((2, CELL, TS), F32),
            pltpu.VMEM((2, 16, 8 * TS), F32),
            pltpu.VMEM((EXT, 3 * TS), F32),
            pltpu.VMEM((KS, EXT, TS), F32),
            pltpu.VMEM((EXT, TS), F32),
            pltpu.VMEM((NB, 2 * TS, TS), F32),
            dma((7,)),
            dma,
            dma((3,)),
            dma((2,)),
            dma((2,)),
            dma((STEPS, 8)),
            dma((STEPS, 8)),
            dma((STEPS, 3, 2)),
            dma((STEPS, 3, 2)),
            dma((STEPS,)),
            dma((STEPS,)),
            dma((STEPS, 4)),
            dma((STEPS, 4)),
            dma((3, 2)),
            dma((3, 2)),
            dma((3,)),
            dma((2,)),
        ],
        compiler_params=pltpu.CompilerParams(
            collective_id=0, has_side_effects=True, vmem_limit_bytes=58 * 2**20
        ),
        name="exchange",
    )(
        index,
        warp_shift.T,
        jnp.transpose(warp_taps, (1, 2, 0)),
        tile_weights,
        meta,
        basis_rows,
        basis_cols,
        raw_tiles,
        template,
    )


def solution(mesh):
    return jax.shard_map(
        body,
        mesh=mesh,
        in_specs=(
            P(("visit", "sky"), None, None),
            P(("visit", "sky"), None),
            P(("visit", "sky"), None, None),
            P(("visit", "sky"), None),
            P(("visit", "sky")),
            P(("visit", "sky"), None),
            P(("visit", "sky")),
            P("sky", None),
            P(),
            P(),
        ),
        out_specs=P("sky", "visit"),
        check_vma=False,
    )
```
